32 devices in a mesh: row: 8 (over z, x), col: 4 (over y, core).
Axes of the slice: x: 2, y: 2, z: 4, core: 2. Of those that a mesh axis runs over, the one named last changes fastest.
Arguments:
- tokens: bfloat16 [192, 8192], P('col', 'row'), may hold values from -6 to 6
- out_grad: bfloat16 [192, 8192], P('col', 'row'), may hold values from -6 to 6
- gate_weight: bfloat16 [8192, 28672], P('row', 'col'), may hold values from -0.0625 to 0.0625
- up_weight: bfloat16 [8192, 28672], P('row', 'col'), may hold values from -0.0625 to 0.0625
- down_weight: bfloat16 [28672, 8192], P('col', 'row'), may hold values from -0.03125 to 0.03125
Outputs:
- input_grad: bfloat16 [192, 8192], P('col', 'row')
- gate_grad: bfloat16 [8192, 28672], P('row', 'col')
- up_grad: bfloat16 [8192, 28672], P('row', 'col')
- down_grad: bfloat16 [28672, 8192], P('col', 'row')
The draws below stay inside these ranges and needn't reach their ends.
All inputs are finite; a program needn't handle non-finite values.
Results may differ from the reference program's by a relative error of at most 0.02.
Values may be sent and summed in bfloat16 or wider, within the bound.
A program may use at most 192 MiB of HBM per device.

```python
import jax
import jax.numpy as jnp
from jax import lax

D = 8192
FF = 28672
TOKENS = 192
N_ROW = 8


def level_of(key, dims, shards, smallest, high):
    def one(dim, blocks):
        heights = jax.random.uniform(jax.random.fold_in(jax.random.fold_in(key, 6), dim), (blocks,), jnp.float32, smallest / len(shards), high / len(shards))
        return jnp.repeat(jnp.exp(heights), dims[dim] // blocks).reshape((-1,) + (1,) * (len(dims) - dim - 1))

    level = one(*shards[0])
    for cut in shards[1:]:
        level = level * one(*cut)
    return level


def centred(own_key, shape, spread, reach, shards=(), held_as=jnp.bfloat16):
    result = jax.random.normal(own_key, shape, jnp.float32) * spread
    if len(shards) > 0:
        result = level_of(own_key, shape, shards, -0.22, 0.18) * result
    return jnp.clip(result, min=-reach, max=reach).astype(held_as)


def setup_inputs(seed: int = 0) -> dict:
    splits = jax.random.split(jax.random.key(seed), 6)
    tokens = centred(splits[0], (TOKENS, D), 1.0, 6.0, ((0, 4), (1, 8)))
    out_grad = centred(splits[1], (TOKENS, D), 1.0, 6.0, ((0, 4), (1, 8)))
    gate_weight = centred(splits[2], (D, FF), D ** -0.5, 0.0625, ((0, 8), (1, 4)))
    up_weight = centred(splits[3], (D, FF), D ** -0.5, 0.0625, ((0, 8), (1, 4)))
    down_weight = centred(splits[4], (FF, D), FF ** -0.5, 0.03125, ((0, 4), (1, 8)))
    return dict(tokens=tokens, out_grad=out_grad, gate_weight=gate_weight, up_weight=up_weight, down_weight=down_weight)


def swiglu_back(gate, up_sum, hidden_delta):
    sigmoid = jax.nn.sigmoid(gate)
    activated = gate * sigmoid
    hidden = (activated * up_sum).astype(jnp.bfloat16)
    up_delta = (hidden_delta * activated).astype(jnp.bfloat16)
    gate_delta = (hidden_delta * up_sum * sigmoid * (1.0 + gate * (1.0 - sigmoid))).astype(jnp.bfloat16)
    return hidden, gate_delta, up_delta


def rounded(value):
    return lax.optimization_barrier(value.astype(jnp.bfloat16)).astype(jnp.float32)


def reference(tokens, out_grad, gate_weight, up_weight, down_weight):
    width = D // N_ROW

    def add_block(totals, block_index):
        first_row = (block_index * width).astype(jnp.int32)
        tok_cols = lax.dynamic_slice_in_dim(tokens, first_row, width, 1)
        grad_cols = lax.dynamic_slice_in_dim(out_grad, first_row, width, 1)
        gate_rows = lax.dynamic_slice_in_dim(gate_weight, first_row, width, 0)
        up_rows = lax.dynamic_slice_in_dim(up_weight, first_row, width, 0)
        down_cols = lax.dynamic_slice_in_dim(down_weight, first_row, width, 1)
        gate_part = rounded(jnp.dot(tok_cols, gate_rows, preferred_element_type=jnp.float32))
        up_part = rounded(jnp.dot(tok_cols, up_rows, preferred_element_type=jnp.float32))
        delta_part = rounded(lax.dot_general(grad_cols, down_cols, (((1,), (1,)), ((), ())), preferred_element_type=jnp.float32))
        return (totals[0] + gate_part, totals[1] + up_part, totals[2] + delta_part), None

    empty = jnp.zeros((TOKENS, FF), jnp.float32)
    totals, _ = lax.scan(add_block, (empty, empty, empty), jnp.arange(N_ROW, dtype=jnp.int32))
    hidden, gate_delta, up_delta = swiglu_back(totals[0], totals[1], totals[2])
    contract_rows = (((0,), (0,)), ((), ()))
    gate_grad = lax.dot_general(tokens, gate_delta, contract_rows, preferred_element_type=jnp.float32).astype(jnp.bfloat16)
    up_grad = lax.dot_general(tokens, up_delta, contract_rows, preferred_element_type=jnp.float32).astype(jnp.bfloat16)
    down_grad = lax.dot_general(hidden, out_grad, contract_rows, preferred_element_type=jnp.float32).astype(jnp.bfloat16)
    contract_cols = (((1,), (1,)), ((), ()))
    input_grad = lax.dot_general(gate_delta, gate_weight, contract_cols, preferred_element_type=jnp.float32)
    input_grad = input_grad + lax.dot_general(up_delta, up_weight, contract_cols, preferred_element_type=jnp.float32)
    return input_grad.astype(jnp.bfloat16), gate_grad, up_grad, down_grad
```

```python
import functools

import jax
import jax.numpy as jnp
from jax import lax
from jax.experimental import pallas as pl
from jax.experimental.pallas import tpu as pltpu
from jax.sharding import PartitionSpec as P

OUTER = 4
CHUNKS = 7
F32, BF16 = jnp.float32, jnp.bfloat16
CONTRACT_COLS = (((1,), (1,)), ((), ()))
CONTRACT_ROWS = (((0,), (0,)), ((), ()))


def swiglu_back(gate, up_sum, hidden_delta):
    sigmoid = jax.nn.sigmoid(gate)
    activated = gate * sigmoid
    hidden = (activated * up_sum).astype(BF16)
    up_delta = (hidden_delta * activated).astype(BF16)
    gate_delta = (hidden_delta * up_sum * sigmoid * (1.0 + gate * (1.0 - sigmoid))).astype(BF16)
    return (hidden, gate_delta, up_delta)


def exchange(
    n_row, tok, grad, gate_w, up_w, down_w, out, in_grad,
    part, from_in, line, from_out, gate_buf, up_buf, down_buf, gate_two, up_two, acc,
    load_sem, two_sem, in_send, in_recv, out_send, out_recv, back_send, back_recv, wide_send, wide_recv,
):
    inner = n_row // OUTER
    total = tok.shape[0]
    rows = total // inner
    high = rows // 2
    half = out.shape[3]
    cols = half // CHUNKS
    me = lax.axis_index("row")
    mo, mi = me // inner, me % inner

    def row_of(o, i):
        return {"row": o * inner + i}

    def peer_in(s):
        return lax.rem(mi + s, inner)

    def peer_out(s):
        return lax.rem(mo + s, OUTER)

    def band(i):
        return pl.ds(pl.multiple_of(i * rows, rows), rows)

    def span(c):
        return pl.ds(pl.multiple_of(c * cols, cols), cols)

    def loads(c):
        slot = lax.rem(c, 2)
        made = []
        for h in range(2):
            at = pl.ds(pl.multiple_of(h * half + c * cols, cols), cols)
            for n, (src, dst) in enumerate(
                [
                    (gate_w.at[:, at], gate_buf.at[slot, h]),
                    (up_w.at[:, at], up_buf.at[slot, h]),
                    (down_w.at[at, :], down_buf.at[slot, h]),
                ]
            ):
                made.append(pltpu.make_async_copy(src, dst, load_sem.at[slot, 3 * h + n]))
        return made

    def loads_two(c):
        made = []
        for h in range(2):
            at = pl.ds(pl.multiple_of(h * half + c * cols, cols), cols)
            made.append(pltpu.make_async_copy(gate_w.at[:, at], gate_two.at[h], two_sem.at[h]))
            made.append(pltpu.make_async_copy(up_w.at[:, at], up_two.at[h], two_sem.at[2 + h]))
        return made

    def send_in(c, s):
        return pltpu.make_async_remote_copy(
            part.at[c, :, :, band(peer_in(s))], from_in.at[s - 1, c],
            in_send.at[s - 1, c], in_recv.at[s - 1, c], device_id=row_of(mo, peer_in(s)),
        )

    def send_out(c, s):
        o = peer_out(s)
        src = line.at[c, :, o % 2, pl.ds(pl.multiple_of(o // 2 * high, high), high)]
        return pltpu.make_async_remote_copy(
            src, from_out.at[s - 1, c],
            out_send.at[s - 1, c], out_recv.at[s - 1, c], device_id=row_of(o, mi),
        )

    my_rows = pl.ds(pl.multiple_of(mi * rows + mo // 2 * high, high), high)

    def send_back(c, s):
        here = out.at[:, mo % 2, my_rows, span(c)]
        return pltpu.make_async_remote_copy(
            here, here, back_send.at[s - 1, c], back_recv.at[s - 1, c],
            device_id=row_of(peer_out(s), mi),
        )

    def send_wide(c, s):
        here = out.at[:, :, band(mi), span(c)]
        return pltpu.make_async_remote_copy(
            here, here, wide_send.at[s - 1, c], wide_recv.at[s - 1, c],
            device_id=row_of(mo, peer_in(s)),
        )

    for copy in loads(0):
        copy.start()
    barrier = pltpu.get_barrier_semaphore()
    for s in range(1, inner):
        pl.semaphore_signal(barrier, inc=1, device_id=row_of(mo, peer_in(s)))
    for s in range(1, OUTER):
        pl.semaphore_signal(barrier, inc=1, device_id=row_of(peer_out(s), mi))
    pl.semaphore_wait(barrier, inner - 1 + OUTER - 1)

    acc[...] = jnp.zeros_like(acc)

    def step(t, carry):
        @pl.when(t >= 4)
        def _():
            for copy in loads_two(t - 4):
                copy.start()

        @pl.when(t < CHUNKS)
        def _():
            c = t
            slot = lax.rem(c, 2)

            @pl.when(c + 1 < CHUNKS)
            def _():
                for copy in loads(c + 1):
                    copy.start()

            for copy in loads(c):
                copy.wait()
            for h in range(2):
                part[c, 0, h] = jnp.dot(
                    tok[...], gate_buf[slot, h], preferred_element_type=F32
                ).astype(BF16)
                part[c, 1, h] = jnp.dot(
                    tok[...], up_buf[slot, h], preferred_element_type=F32
                ).astype(BF16)
                part[c, 2, h] = lax.dot_general(
                    grad[...], down_buf[slot, h], CONTRACT_COLS, preferred_element_type=F32
                ).astype(BF16)
            for s in range(1, inner):
                send_in(c, s).start()

        @pl.when((t >= 1) & (t < CHUNKS + 1))
        def _():
            c = t - 1
            for s in range(1, inner):
                send_in(c, s).wait_recv()
            for k in range(3):
                for h in range(2):
                    value = part[c, k, h, band(mi)].astype(F32)
                    for s in range(1, inner):
                        value = value + from_in[s - 1, c, k, h].astype(F32)
                    line[c, k, h] = value.astype(BF16)
            for s in range(1, OUTER):
                send_out(c, s).start()

        @pl.when((t >= 2) & (t < CHUNKS + 2))
        def _():
            c = t - 2
            for s in range(1, OUTER):
                send_out(c, s).wait_recv()
            sums = []
            for k in range(3):
                value = line[
                    c, k, mo % 2, pl.ds(pl.multiple_of(mo // 2 * high, high), high)
                ].astype(F32)
                for s in range(1, OUTER):
                    value = value + from_out[s - 1, c, k].astype(F32)
                sums.append(value)
            for k, value in enumerate(swiglu_back(*sums)):
                out[k, mo % 2, my_rows, span(c)] = value
            for s in range(1, OUTER):
                send_back(c, s).start()

        @pl.when((t >= 3) & (t < CHUNKS + 3))
        def _():
            c = t - 3
            for s in range(1, OUTER):
                send_back(c, s).wait_recv()
            for s in range(1, inner):
                send_wide(c, s).start()

        @pl.when(t >= 4)
        def _():
            c = t - 4
            for s in range(1, inner):
                send_wide(c, s).wait_recv()
            for copy in loads_two(c):
                copy.wait()
            for h in range(2):
                acc[...] += lax.dot_general(
                    out[1, h, :, span(c)], gate_two[h], CONTRACT_COLS, preferred_element_type=F32
                ) + lax.dot_general(
                    out[2, h, :, span(c)], up_two[h], CONTRACT_COLS, preferred_element_type=F32
                )

        return carry

    lax.fori_loop(0, CHUNKS + 4, step, 0)
    in_grad[...] = acc[...].astype(BF16)

    def finish(c, carry):
        for s in range(1, inner):
            send_in(c, s).wait_send()
            send_wide(c, s).wait_send()
        for s in range(1, OUTER):
            send_out(c, s).wait_send()
            send_back(c, s).wait_send()
        return carry

    lax.fori_loop(0, CHUNKS, finish, 0)


def grads(tok_t, grad, hidden, gate_delta, up_delta, gate_out, up_out, down_out):
    gate_out[...] = jnp.dot(tok_t[...], gate_delta[0, 0], preferred_element_type=F32).astype(BF16)
    up_out[...] = jnp.dot(tok_t[...], up_delta[0, 0], preferred_element_type=F32).astype(BF16)
    down_out[...] = lax.dot_general(
        hidden[0, 0], grad[...], CONTRACT_ROWS, preferred_element_type=F32
    ).astype(BF16)


def per_device(n_row, tokens, out_grad, gate_weight, up_weight, down_weight):
    inner = n_row // OUTER
    both = lax.all_gather(jnp.stack([tokens, out_grad]), "col", axis=1, tiled=True)
    tok, grad = both[0], both[1]
    total, depth = tok.shape
    width = gate_weight.shape[1]
    half = width // 2
    cols = half // CHUNKS
    rows = total // inner
    dma = pltpu.SemaphoreType.DMA
    vmem = pl.BlockSpec(memory_space=pltpu.VMEM)
    anywhere = pl.BlockSpec(memory_space=pl.ANY)
    every, in_part = pl.pallas_call(
        functools.partial(exchange, n_row),
        out_shape=(
            jax.ShapeDtypeStruct((3, 2, total, half), BF16),
            jax.ShapeDtypeStruct((total, depth), BF16),
        ),
        in_specs=[vmem, vmem, anywhere, anywhere, anywhere],
        out_specs=(vmem, vmem),
        scratch_shapes=[
            pltpu.VMEM((CHUNKS, 3, 2, total, cols), BF16),
            pltpu.VMEM((inner - 1, CHUNKS, 3, 2, rows, cols), BF16),
            pltpu.VMEM((CHUNKS, 3, 2, rows, cols), BF16),
            pltpu.VMEM((OUTER - 1, CHUNKS, 3, rows // 2, cols), BF16),
            pltpu.VMEM((2, 2, depth, cols), BF16),
            pltpu.VMEM((2, 2, depth, cols), BF16),
            pltpu.VMEM((2, 2, cols, depth), BF16),
            pltpu.VMEM((2, depth, cols), BF16),
            pltpu.VMEM((2, depth, cols), BF16),
            pltpu.VMEM((total, depth), F32),
            dma((2, 6)),
            dma((4,)),
            dma((inner - 1, CHUNKS)),
            dma((inner - 1, CHUNKS)),
            dma((OUTER - 1, CHUNKS)),
            dma((OUTER - 1, CHUNKS)),
            dma((OUTER - 1, CHUNKS)),
            dma((OUTER - 1, CHUNKS)),
            dma((inner - 1, CHUNKS)),
            dma((inner - 1, CHUNKS)),
        ],
        compiler_params=pltpu.CompilerParams(
            collective_id=0, has_side_effects=True, vmem_limit_bytes=52 * 2**20
        ),
        cost_estimate=pl.CostEstimate(
            flops=10 * total * depth * width, bytes_accessed=10 * depth * width, transcendentals=0
        ),
    )(tok, grad, gate_weight, up_weight, down_weight)
    input_grad = lax.psum_scatter(in_part, "col", scatter_dimension=0, tiled=True)

    def columns(k):
        return pl.BlockSpec((1, 1, total, cols), lambda n: (k, n // CHUNKS, 0, n % CHUNKS))

    gate_grad, up_grad, down_grad = pl.pallas_call(
        grads,
        grid=(2 * CHUNKS,),
        out_shape=(
            jax.ShapeDtypeStruct((depth, width), BF16),
            jax.ShapeDtypeStruct((depth, width), BF16),
            jax.ShapeDtypeStruct((width, depth), BF16),
        ),
        in_specs=[
            pl.BlockSpec((depth, total), lambda n: (0, 0)),
            pl.BlockSpec((total, depth), lambda n: (0, 0)),
            columns(0),
            columns(1),
            columns(2),
        ],
        out_specs=(
            pl.BlockSpec((depth, cols), lambda n: (0, n)),
            pl.BlockSpec((depth, cols), lambda n: (0, n)),
            pl.BlockSpec((cols, depth), lambda n: (n, 0)),
        ),
        compiler_params=pltpu.CompilerParams(vmem_limit_bytes=40 * 2**20),
        cost_estimate=pl.CostEstimate(
            flops=6 * total * depth * width, bytes_accessed=6 * depth * width, transcendentals=0
        ),
    )(tok.T, grad, every, every, every)
    return (input_grad, gate_grad, up_grad, down_grad)


def solution(mesh):
    return jax.shard_map(
        functools.partial(per_device, mesh.shape["row"]),
        mesh=mesh,
        in_specs=(
            P("col", "row"),
            P("col", "row"),
            P("row", "col"),
            P("row", "col"),
            P("col", "row"),
        ),
        out_specs=(P("col", "row"), P("row", "col"), P("row", "col"), P("col", "row")),
        check_vma=False,
    )
```
